32 devices in a mesh: groups: 2 (over y), sec: 4 (over z), env: 2 (over x), rep: 2 (over core).
Axes of the slice: x: 2, y: 2, z: 4, core: 2. Of those that a mesh axis runs over, the one named last changes fastest.
Arguments:
- wavefunction: bfloat16 [32, 256, 256], P(('groups', 'sec'), None, 'rep'), parts along dimension 0, may hold values from -6 to 6
- left_env: bfloat16 [8, 8, 256, 256], P(('groups', 'env'), 'sec'), parts along dimension 0, may hold values from -0.078125 to 0.078125
- right_env: bfloat16 [8, 16, 256, 256], P(('groups', 'env'), 'sec', 'rep'), parts along dimension 0, may hold values from -0.375 to 0.375
- left_index: int32 [8, 16, 6], P(('groups', 'env'), 'sec'), parts along dimension 0, may hold values from 0 to 7
- out_sector: int32 [8, 16, 6], P(('groups', 'env'), 'sec'), parts along dimension 0, may hold values from 0 to 15, as said below
Outputs:
- product: float32 [32, 256, 256], P(('groups', 'sec'), None, 'rep'), parts along dimension 0
The draws below stay inside these ranges and needn't reach their ends.
There are 2 independent parts, one for each index of `groups`. The reference program is written for one: setup_inputs(seed, part) draws one part's arguments, and reference() takes and returns one part's arrays. A program takes and returns all parts, laid end to end along the dimension named above; each array names one. Nothing has to cross between parts.
Inputs may be any that keep to these rules, and one draw needn't show every extreme that they name: `out_sector`: group the pairs by device: those with terms of one index of env and input sectors of one index of sec. The output sectors named by such a group are 5 distinct ones, of which at most 2 belong to the sectors of any one index of sec, and exactly 2 to some index.
All inputs are finite; a program needn't handle non-finite values.
Results may differ from the reference program's by a relative error of at most 0.0029.
Values may be sent and summed in bfloat16 or wider, within the bound.
A program may use at most 64 MiB of HBM per device.

```python
import jax
import jax.numpy as jnp
from jax import lax

BLOCK = 256
SEC_DEV = 4
TERM_DEV = 2
OUTS = 6
CAP_OUT = 2
SECTORS = 16
TERMS = 4
NBLOCKS = 8
TARGETS_DEV = 5
N_SEC = 4
N_ENV = 2


def device_targets(key):
    keys = jax.random.split(key, 5)
    pair_total = TERM_DEV * SEC_DEV * OUTS
    leading = jax.random.randint(keys[0], (), 0, N_SEC)
    others = (leading + 1 + jnp.arange((N_SEC - 1) * CAP_OUT) // CAP_OUT) % N_SEC
    others = jax.random.permutation(keys[1], others)[:TARGETS_DEV - CAP_OUT]
    owners = jnp.concatenate([jnp.full((CAP_OUT,), leading, jnp.int32), others.astype(jnp.int32)])
    positions = jnp.arange(TARGETS_DEV)
    earlier = positions[None, :] < positions[:, None]
    slot_rank = jnp.sum((owners[None, :] == owners[:, None]) & earlier, axis=1).astype(jnp.int32)
    offsets = jax.random.randint(keys[2], (N_SEC,), 0, SEC_DEV)
    local_ids = (offsets[owners] + slot_rank) % SEC_DEV
    targets = owners * SEC_DEV + local_ids
    extra = jax.random.randint(keys[3], (pair_total - TARGETS_DEV,), 0, TARGETS_DEV)
    picks = jnp.concatenate([jnp.arange(TARGETS_DEV).astype(jnp.int32), extra.astype(jnp.int32)])
    picks = jax.random.permutation(keys[4], picks)
    return targets[picks].astype(jnp.int32)


def draw_out_sector(key, part):
    key = jax.random.fold_in(key, 11)
    device_keys = jax.random.split(key, N_ENV * N_SEC)
    rows = jax.vmap(device_targets)(device_keys)
    rows = rows.reshape(N_ENV, N_SEC, TERM_DEV, SEC_DEV, OUTS)
    rows = jnp.transpose(rows, (0, 2, 1, 3, 4))
    return rows.reshape(TERMS, SECTORS, OUTS).astype(jnp.int32)


def set_ends(array, rng, least, largest):
    longest = array.shape.index(max(array.shape))
    spots = []
    for shift in (0, 1):
        where = [jax.random.randint(jax.random.fold_in(rng, axis), (), 0, length) for axis, length in enumerate(array.shape)]
        where[longest] = (where[longest] + shift) % array.shape[longest]
        spots.append(tuple(where))
    return array.at[spots[0]].set(least).at[spots[1]].set(largest)


def levels(own_key, dims, cuts, least, high):
    gain = 1.0
    for dim, parts in cuts:
        heights = jax.random.uniform(jax.random.fold_in(jax.random.fold_in(own_key, 6), dim), (parts,), jnp.float32, least / len(cuts), high / len(cuts))
        gain = gain * jnp.repeat(jnp.exp(heights), dims[dim] // parts).reshape((-1,) + (1,) * (len(dims) - 1 - dim))
    return gain


def normal_values(stream_key, dims, scale, reach, shards=(), held_as=jnp.bfloat16):
    drawn = scale * jax.random.normal(stream_key, dims, jnp.float32)
    if shards:
        drawn = drawn * levels(stream_key, dims, shards, -0.22, 0.18)
    return jnp.clip(drawn, -reach, reach).astype(held_as)


def setup_inputs(seed: int = 0, part: int = 0) -> dict:
    splits = jax.random.split(jax.random.key(seed), 6)
    part_splits = jax.random.split(jax.random.fold_in(splits[5], part), 6)
    wavefunction = normal_values(part_splits[0], (SECTORS, BLOCK, BLOCK), 1.0, 6.0, ((0, 4), (2, 2)))
    left_env = normal_values(part_splits[1], (TERMS, NBLOCKS, BLOCK, BLOCK), (BLOCK * TERMS * OUTS) ** -0.5, 0.078125, ((0, 2), (1, 4)))
    right_env = normal_values(part_splits[2], (TERMS, SECTORS, BLOCK, BLOCK), BLOCK ** -0.5, 0.375, ((0, 2), (1, 4), (2, 2)))
    left_index = set_ends(jax.random.randint(part_splits[3], (TERMS, SECTORS, OUTS), 0, NBLOCKS), jax.random.fold_in(part_splits[3], 1), 0, NBLOCKS - 1).astype(jnp.int32)
    out_sector = draw_out_sector(jax.random.fold_in(jax.random.fold_in(splits[5], part), 71), part)
    return dict(wavefunction=wavefunction, left_env=left_env, right_env=right_env, left_index=left_index, out_sector=out_sector)


def reference(wavefunction, left_env, right_env, left_index, out_sector):
    wave_wide = wavefunction.astype(jnp.float32)

    def add_term(result_sum, inputs):
        left_term, right_term, index_term, target_term = inputs
        right_products = jnp.einsum('sij,srj->sir', wave_wide, right_term.astype(jnp.float32)).astype(jnp.bfloat16)
        products_wide = right_products.astype(jnp.float32)

        def add_column(inner_sum, column_data):
            block_ids, targets = column_data
            chosen = left_term[block_ids].astype(jnp.float32)
            pair_block = jnp.einsum('sij,sjl->sil', chosen, products_wide)
            return inner_sum.at[targets].add(pair_block), None

        result_sum, unused = lax.scan(add_column, result_sum, (index_term.T, target_term.T))
        return result_sum, None

    initial = jnp.zeros((SECTORS, BLOCK, BLOCK), jnp.float32)
    product, unused = lax.scan(add_term, initial, (left_env, right_env, left_index, out_sector))
    return product
```

```python
import functools

import jax
import jax.numpy as jnp
from jax import lax
from jax.experimental import pallas as pl
from jax.experimental.pallas import tpu as pltpu
from jax.sharding import PartitionSpec as P

MESH = pl.DeviceIdType.MESH
SLOTS = 2
CHUNKS = 1


def kernel(dims, *refs):
    n, n_env, chunks, terms, sectors, blocks, outs = dims
    wave_ref, left_ref, right_ref, lidx_ref, osec_ref, out_ref = refs[:6]
    refs = list(refs[6:])
    wave_all, prods, chain, lab_send, lab_recv, dense_own, prev_s, last_s = refs[:8]
    refs = refs[8:]
    left_all = refs[:chunks]
    slot_send = refs[chunks : 2 * chunks]
    slot_recv = refs[2 * chunks : 3 * chunks]
    env_all = refs[3 * chunks : 4 * chunks]
    (up_s, up_r, dn_s, dn_r, sib_s, sib_r, w_s, w_r, sl_s, sl_r, lb_s, lb_r, ev_s, ev_r, loc) = refs[4 * chunks :]
    me = lax.axis_index("sec")
    env = lax.axis_index("env")
    core = lax.axis_index("rep")
    per = terms * blocks
    pairs = terms * sectors * outs
    rows = left_ref.shape[2] * left_ref.shape[3]
    width = wave_ref.shape[-1]

    barrier = pltpu.get_barrier_semaphore()
    for d in range(1, n):
        pl.semaphore_signal(barrier, inc=1, device_id={"sec": lax.rem(me + d, n)}, device_id_type=MESH)
    for d in range(1, n_env):
        pl.semaphore_signal(barrier, inc=1, device_id={"env": lax.rem(env + d, n_env)}, device_id_type=MESH)
    pl.semaphore_signal(barrier, inc=1, device_id={"rep": 1 - core}, device_id_type=MESH)
    pl.semaphore_wait(barrier, n - 1 + n_env - 1 + 1)

    def remote(src, dst, send, recv, where):
        return pltpu.make_async_remote_copy(
            src_ref=src, dst_ref=dst, send_sem=send, recv_sem=recv, device_id=where, device_id_type=MESH
        )

    def piece(r, origin):
        return left_all[r].at[pl.ds(origin * per, per), core]

    def hop(r, s, up, origin):
        src = left_ref.at[:, r, core] if s == 0 else piece(r, origin)
        send, recv = (up_s, up_r) if up else (dn_s, dn_r)
        where = jnp.minimum(me + 1, n - 1) if up else jnp.maximum(me - 1, 0)
        return remote(src, piece(r, origin), send.at[r, s], recv.at[r, s], {"sec": where})

    def sibling(r, origin, half):
        ref = left_all[r].at[pl.ds(origin * per, per), half]
        return remote(ref, ref, sib_s.at[r, origin], sib_r.at[r, origin], {"rep": 1 - core})

    def begin(r):
        @pl.when(me + 1 < n)
        def _():
            hop(r, 0, True, me).start()

        @pl.when(me > 0)
        def _():
            hop(r, 0, False, me).start()

    def relay(r):
        for s in range(n - 1):
            @pl.when(me - 1 - s >= 0)
            def _():
                origin = me - 1 - s
                hop(r, s, True, origin).wait_recv()
                if s + 1 <= n - 2:
                    @pl.when(me + 1 < n)
                    def _():
                        hop(r, s + 1, True, origin).start()
                sibling(r, origin, core).start()

            @pl.when(me + 1 + s <= n - 1)
            def _():
                origin = me + 1 + s
                hop(r, s, False, origin).wait_recv()
                if s + 1 <= n - 2:
                    @pl.when(me > 0)
                    def _():
                        hop(r, s + 1, False, origin).start()
                sibling(r, origin, core).start()

    def gathered(r):
        for d in range(1, n):
            sibling(r, lax.rem(me + d, n), 1 - core).wait_recv()

    begin(0)
    wave_copy = remote(wave_ref, wave_all.at[core], w_s, w_r, {"rep": 1 - core})
    wave_copy.start()
    own_copies = [
        pltpu.make_async_copy(left_ref.at[:, r], left_all[r].at[pl.ds(me * per, per)], loc.at[r])
        for r in range(chunks)
    ]
    for copy in own_copies:
        copy.start()
    wave_all[core] = wave_ref[...]

    def find_prev(p, carry):
        target = osec_ref[p]
        found = jnp.int32(pairs)
        for q in range(pairs - 1):
            found = jnp.where((osec_ref[q] == target) & (q < p), q, found)
        prev_s[p] = found
        return carry

    lax.fori_loop(0, pairs, find_prev, 0)

    def find_last(v, carry):
        found = jnp.int32(-1)
        for q in range(pairs):
            found = jnp.where(osec_ref[q] == v, q, found)
        last_s[v] = found
        return carry

    lax.fori_loop(0, n * sectors, find_last, 0)

    def slot_of(owner, i):
        low, high = jnp.int32(-1), jnp.int32(-1)
        for l in range(sectors):
            here = last_s[owner * sectors + l] >= 0
            high = jnp.where(here, l, high)
            low = jnp.where(here & (low < 0), l, low)
        label = low if i == 0 else jnp.where(high == low, -1, high)
        source = jnp.where(label >= 0, last_s[owner * sectors + jnp.maximum(label, 0)], pairs)
        return label, source

    def write_labels(owner, carry):
        for i in range(SLOTS):
            lab_send[owner, i] = jnp.full((8, 128), slot_of(owner, i)[0], jnp.int32)
        return carry

    lax.fori_loop(0, n, write_labels, 0)

    def label_copy(d):
        owner = lax.rem(me + d, n)
        return remote(lab_send.at[owner], lab_recv.at[me], lb_s.at[d], lb_r.at[d], {"sec": owner})

    for d in range(1, n):
        label_copy(d).start()
    wave_copy.wait()

    for s in range(sectors):
        wave = jnp.concatenate([wave_all[0, s], wave_all[1, s]], axis=-1)
        for k in range(terms):
            prods[k * sectors + s] = lax.dot_general(
                wave, right_ref[k, s], (((1,), (1,)), ((), ())), preferred_element_type=jnp.float32
            ).astype(jnp.bfloat16)
    chain[pairs] = jnp.zeros((rows, width), jnp.float32)

    def compute(r):
        def body(ks, carry):
            k = ks // sectors
            right = prods[ks]
            for m in range(outs):
                p = ks * outs + m
                b = lidx_ref[p]
                left = left_all[r][(b // blocks) * per + k * blocks + lax.rem(b, blocks)]
                value = jnp.dot(left.reshape(rows, -1), right, preferred_element_type=jnp.float32)
                chain[p] = value + chain[prev_s[p]]
            return carry

        lax.fori_loop(0, terms * sectors, body, 0)

    def slot_copy(r, d):
        owner = lax.rem(me + d, n)
        return remote(
            slot_send[r].at[pl.ds(owner * SLOTS, SLOTS)],
            slot_recv[r].at[pl.ds(me * SLOTS, SLOTS)],
            sl_s.at[r, d],
            sl_r.at[r, d],
            {"sec": owner},
        )

    def send_slots(r):
        for d in range(n - 1, 0, -1):
            owner = lax.rem(me + d, n)
            for i in range(SLOTS):
                slot_send[r][owner * SLOTS + i] = chain[slot_of(owner, i)[1]].astype(jnp.bfloat16)
            slot_copy(r, d).start()
        labels = [slot_of(me, i) for i in range(SLOTS)]
        parts = [chain[source] for _, source in labels]
        for l in range(sectors):
            total = jnp.zeros((rows, width), jnp.float32)
            for i in range(SLOTS):
                total = total + jnp.where(labels[i][0] == l, parts[i], 0.0)
            dense_own[r, l] = total

    def env_copy(r, d):
        peer = lax.rem(env + d, n_env)
        ref = env_all[r].at[env]
        return remote(ref, ref, ev_s.at[r, d], ev_r.at[r, d], {"env": peer})

    def sum_slots(r):
        for d in range(1, n):
            slot_copy(r, d).wait_recv()
        for l in range(sectors):
            total = dense_own[r, l]
            for d in range(1, n):
                source = lax.rem(me + d, n)
                for i in range(SLOTS):
                    mask = lab_recv[source, i][:1] == l
                    total = total + jnp.where(mask, slot_recv[r][source * SLOTS + i].astype(jnp.float32), 0.0)
            env_all[r][env, l] = total.astype(env_all[r].dtype)
        for d in range(1, n_env):
            env_copy(r, d).start()

    def finish(r):
        for d in range(1, n_env):
            env_copy(r, d).wait_recv()
        for l in range(sectors):
            total = env_all[r][0, l].astype(jnp.float32)
            for e in range(1, n_env):
                total = total + env_all[r][e, l].astype(jnp.float32)
            out_ref[l, r * rows : (r + 1) * rows] = total

    for r in range(chunks):
        relay(r)
        if r + 1 < chunks:
            begin(r + 1)
        gathered(r)
        own_copies[r].wait()
        compute(r)
        send_slots(r)
        if r == 1:
            for d in range(1, n):
                label_copy(d).wait_recv()
        if r >= 1:
            sum_slots(r - 1)
        if r >= 2:
            finish(r - 2)
    if chunks == 1:
        for d in range(1, n):
            label_copy(d).wait_recv()
    sum_slots(chunks - 1)
    for r in range(max(chunks - 2, 0), chunks):
        finish(r)

    for r in range(chunks):
        for s in range(n - 1):
            @pl.when((me - s >= 0) & (me + 1 < n))
            def _():
                hop(r, s, True, me - s).wait_send()

            @pl.when((me + s <= n - 1) & (me > 0))
            def _():
                hop(r, s, False, me + s).wait_send()
        for d in range(1, n):
            sibling(r, lax.rem(me + d, n), core).wait_send()
            slot_copy(r, d).wait_send()
        for d in range(1, n_env):
            env_copy(r, d).wait_send()
    for d in range(1, n):
        label_copy(d).wait_send()


def on_device(n, n_env, wavefunction, left_env, right_env, left_index, out_sector):
    sectors, height, width = wavefunction.shape
    terms, blocks = left_env.shape[:2]
    outs = left_index.shape[-1]
    chunks = CHUNKS
    rows = height // chunks
    pairs = terms * sectors * outs
    per = terms * blocks
    bf16, f32 = jnp.bfloat16, jnp.float32
    left = left_env.reshape(per, chunks, 2, rows // 2, height)
    vmem = pl.BlockSpec(memory_space=pltpu.VMEM)
    smem = pl.BlockSpec(memory_space=pltpu.SMEM)
    dma = pltpu.SemaphoreType.DMA
    scratch = [
        pltpu.VMEM((2, sectors, height, width), bf16),
        pltpu.VMEM((terms * sectors, height, width), bf16),
        pltpu.VMEM((pairs + 1, rows, width), f32),
        pltpu.VMEM((n, SLOTS, 8, 128), jnp.int32),
        pltpu.VMEM((n, SLOTS, 8, 128), jnp.int32),
        pltpu.VMEM((chunks, sectors, rows, width), f32),
        pltpu.SMEM((pairs,), jnp.int32),
        pltpu.SMEM((n * sectors,), jnp.int32),
    ]
    scratch += [pltpu.VMEM((n * per, 2, rows // 2, height), bf16)] * chunks
    scratch += [pltpu.VMEM((n * SLOTS, rows, width), bf16)] * (2 * chunks)
    scratch += [pltpu.VMEM((n_env, sectors, rows, width), bf16)] * chunks
    scratch += [dma((chunks, n - 1))] * 4 + [dma((chunks, n))] * 2 + [dma, dma]
    scratch += [dma((chunks, n))] * 2 + [dma((n,))] * 2 + [dma((chunks, n_env))] * 2 + [dma((chunks,))]
    dims = (n, n_env, chunks, terms, sectors, blocks, outs)
    return pl.pallas_call(
        functools.partial(kernel, dims),
        out_shape=jax.ShapeDtypeStruct(wavefunction.shape, f32),
        in_specs=[vmem, vmem, vmem, smem, smem],
        out_specs=vmem,
        scratch_shapes=scratch,
        compiler_params=pltpu.CompilerParams(
            collective_id=0, has_side_effects=True, vmem_limit_bytes=48 * 1024 * 1024
        ),
    )(wavefunction, left, right_env, left_index.reshape(-1), out_sector.reshape(-1))


def solution(mesh):
    in_specs = (
        P(("groups", "sec"), None, "rep"),
        P(("groups", "env"), "sec", None, None),
        P(("groups", "env"), "sec", "rep", None),
        P(("groups", "env"), "sec", None),
        P(("groups", "env"), "sec", None),
    )
    out_specs = P(("groups", "sec"), None, "rep")
    return jax.shard_map(
        functools.partial(on_device, mesh.shape["sec"], mesh.shape["env"]),
        mesh=mesh,
        in_specs=in_specs,
        out_specs=out_specs,
        check_vma=False,
    )
```

```python
import functools

import jax
import jax.numpy as jnp
from jax import lax
from jax.experimental import pallas as pl
from jax.experimental.pallas import tpu as pltpu
from jax.sharding import PartitionSpec as P

MESH = pl.DeviceIdType.MESH
SLOTS = 2
CHUNKS = 1
PARTS = 4


def kernel(dims, *refs):
    n, n_env, chunks, parts, terms, sectors, blocks, outs = dims
    units = chunks * parts
    wave_ref, left_ref, right_hbm, lidx_in, osec_in, out_ref = refs[:6]
    refs = list(refs[6:])
    wave_all, right_ref, prods, chain, lab_send, lab_recv, dense_own, prev_s, last_s, lidx_s, osec_s, lidx_ref, osec_ref = refs[:13]
    refs = refs[13:]
    left_all = refs[:chunks]
    refs = refs[chunks:]
    slot_send = refs[:units]
    slot_recv = refs[units : 2 * units]
    env_all = refs[2 * units : 3 * units]
    (up_s, up_r, dn_s, dn_r, sib_s, sib_r, w_s, w_r, sl_s, sl_r, lb_s, lb_r, ev_s, ev_r, loc) = refs[3 * units :]
    me = lax.axis_index("sec")
    env = lax.axis_index("env")
    core = lax.axis_index("rep")
    per = terms * blocks
    pairs = terms * sectors * outs
    rows = left_ref.shape[2] * left_ref.shape[3] // parts
    width = wave_ref.shape[-1]

    barrier = pltpu.get_barrier_semaphore()
    for d in range(1, n):
        pl.semaphore_signal(barrier, inc=1, device_id={"sec": lax.rem(me + d, n)}, device_id_type=MESH)
    for d in range(1, n_env):
        pl.semaphore_signal(barrier, inc=1, device_id={"env": lax.rem(env + d, n_env)}, device_id_type=MESH)
    pl.semaphore_signal(barrier, inc=1, device_id={"rep": 1 - core}, device_id_type=MESH)
    pl.semaphore_wait(barrier, n - 1 + n_env - 1 + 1)

    def remote(src, dst, send, recv, where):
        return pltpu.make_async_remote_copy(
            src_ref=src, dst_ref=dst, send_sem=send, recv_sem=recv, device_id=where, device_id_type=MESH
        )

    def piece(r, origin):
        return left_all[r].at[pl.ds(origin * per, per), core]

    def hop(r, s, up, origin):
        src = left_ref.at[:, r, core] if s == 0 else piece(r, origin)
        send, recv = (up_s, up_r) if up else (dn_s, dn_r)
        where = jnp.minimum(me + 1, n - 1) if up else jnp.maximum(me - 1, 0)
        return remote(src, piece(r, origin), send.at[r, s], recv.at[r, s], {"sec": where})

    def sibling(r, origin, half):
        ref = left_all[r].at[pl.ds(origin * per, per), half]
        return remote(ref, ref, sib_s.at[r, origin], sib_r.at[r, origin], {"rep": 1 - core})

    def begin(r):
        @pl.when(me + 1 < n)
        def _():
            hop(r, 0, True, me).start()

        @pl.when(me > 0)
        def _():
            hop(r, 0, False, me).start()

    def relay(r):
        for s in range(n - 1):
            @pl.when(me - 1 - s >= 0)
            def _():
                origin = me - 1 - s
                hop(r, s, True, origin).wait_recv()
                if s + 1 <= n - 2:
                    @pl.when(me + 1 < n)
                    def _():
                        hop(r, s + 1, True, origin).start()
                sibling(r, origin, core).start()

            @pl.when(me + 1 + s <= n - 1)
            def _():
                origin = me + 1 + s
                hop(r, s, False, origin).wait_recv()
                if s + 1 <= n - 2:
                    @pl.when(me > 0)
                    def _():
                        hop(r, s + 1, False, origin).start()
                sibling(r, origin, core).start()

    def gathered(r):
        for d in range(1, n):
            sibling(r, lax.rem(me + d, n), 1 - core).wait_recv()

    begin(0)
    wave_copy = remote(wave_ref, wave_all.at[core], w_s, w_r, {"rep": 1 - core})
    wave_copy.start()
    own_copies = [
        pltpu.make_async_copy(left_ref.at[:, r], left_all[r].at[pl.ds(me * per, per)], loc.at[r])
        for r in range(chunks)
    ]
    for copy in own_copies:
        copy.start()
    in_copies = [
        pltpu.make_async_copy(wave_ref, wave_all.at[core], loc.at[chunks]),
        pltpu.make_async_copy(right_hbm, right_ref, loc.at[chunks + 1]),
    ]
    index_copies = [
        pltpu.make_async_copy(lidx_in, lidx_s, loc.at[chunks + 2]),
        pltpu.make_async_copy(osec_in, osec_s, loc.at[chunks + 3]),
    ]
    for copy in index_copies + in_copies:
        copy.start()
    for copy in index_copies:
        copy.wait()
    for p in range(pairs):
        k, s, m = p // (sectors * outs), p // outs % sectors, p % outs
        lidx_ref[p] = lidx_s[k, s, m]
        osec_ref[p] = osec_s[k, s, m]

    def find_prev(p, carry):
        target = osec_ref[p]
        found = jnp.int32(pairs)
        for q in range(pairs - 1):
            found = jnp.where((osec_ref[q] == target) & (q < p), q, found)
        prev_s[p] = found
        return carry

    lax.fori_loop(0, pairs, find_prev, 0)

    def find_last(v, carry):
        found = jnp.int32(-1)
        for q in range(pairs):
            found = jnp.where(osec_ref[q] == v, q, found)
        last_s[v] = found
        return carry

    lax.fori_loop(0, n * sectors, find_last, 0)

    def slot_of(owner, i):
        low, high = jnp.int32(-1), jnp.int32(-1)
        for l in range(sectors):
            here = last_s[owner * sectors + l] >= 0
            high = jnp.where(here, l, high)
            low = jnp.where(here & (low < 0), l, low)
        label = low if i == 0 else jnp.where(high == low, -1, high)
        source = jnp.where(label >= 0, last_s[owner * sectors + jnp.maximum(label, 0)], pairs)
        return label, source

    def write_labels(owner, carry):
        for i in range(SLOTS):
            lab_send[owner, i] = jnp.full((8, 128), slot_of(owner, i)[0], jnp.int32)
        return carry

    lax.fori_loop(0, n, write_labels, 0)

    def label_copy(d):
        owner = lax.rem(me + d, n)
        return remote(lab_send.at[owner], lab_recv.at[me], lb_s.at[d], lb_r.at[d], {"sec": owner})

    for d in range(1, n):
        label_copy(d).start()
    wave_copy.wait()
    for copy in in_copies:
        copy.wait()

    for s in range(sectors):
        wave = jnp.concatenate([wave_all[0, s], wave_all[1, s]], axis=-1)
        for k in range(terms):
            prods[k * sectors + s] = lax.dot_general(
                wave, right_ref[k, s], (((1,), (1,)), ((), ())), preferred_element_type=jnp.float32
            ).astype(jnp.bfloat16)
    chain[pairs] = jnp.zeros((rows, width), jnp.float32)

    def compute(u):
        r, t = u // parts, u % parts
        def body(ks, carry):
            k = ks // sectors
            right = prods[ks]
            for m in range(outs):
                p = ks * outs + m
                b = lidx_ref[p]
                left = left_all[r][(b // blocks) * per + k * blocks + lax.rem(b, blocks)]
                value = jnp.dot(left.reshape(rows * parts, -1)[t * rows : (t + 1) * rows], right, preferred_element_type=jnp.float32)
                chain[p] = value + chain[prev_s[p]]
            return carry

        lax.fori_loop(0, terms * sectors, body, 0)

    def slot_copy(r, d):
        owner = lax.rem(me + d, n)
        return remote(
            slot_send[r].at[pl.ds(owner * SLOTS, SLOTS)],
            slot_recv[r].at[pl.ds(me * SLOTS, SLOTS)],
            sl_s.at[r, d],
            sl_r.at[r, d],
            {"sec": owner},
        )

    def send_slots(r):
        for d in range(n - 1, 0, -1):
            owner = lax.rem(me + d, n)
            for i in range(SLOTS):
                slot_send[r][owner * SLOTS + i] = chain[slot_of(owner, i)[1]].astype(jnp.bfloat16)
            slot_copy(r, d).start()
        labels = [slot_of(me, i) for i in range(SLOTS)]
        parts = [chain[source] for _, source in labels]
        for l in range(sectors):
            total = jnp.zeros((rows, width), jnp.float32)
            for i in range(SLOTS):
                total = total + jnp.where(labels[i][0] == l, parts[i], 0.0)
            dense_own[r, l] = total

    def env_copy(r, d):
        peer = lax.rem(env + d, n_env)
        ref = env_all[r].at[env]
        return remote(ref, ref, ev_s.at[r, d], ev_r.at[r, d], {"env": peer})

    def sum_slots(r):
        for d in range(1, n):
            slot_copy(r, d).wait_recv()
        for l in range(sectors):
            total = dense_own[r, l]
            for d in range(1, n):
                source = lax.rem(me + d, n)
                for i in range(SLOTS):
                    mask = lab_recv[source, i][:1] == l
                    total = total + jnp.where(mask, slot_recv[r][source * SLOTS + i].astype(jnp.float32), 0.0)
            env_all[r][env, l] = total.astype(env_all[r].dtype)
        for d in range(1, n_env):
            env_copy(r, d).start()

    def finish(r):
        for d in range(1, n_env):
            env_copy(r, d).wait_recv()
        for l in range(sectors):
            total = env_all[r][0, l].astype(jnp.float32)
            for e in range(1, n_env):
                total = total + env_all[r][e, l].astype(jnp.float32)
            out_ref[l, r * rows : (r + 1) * rows] = total

    summed = 0
    for r in range(chunks):
        relay(r)
        if r + 1 < chunks:
            begin(r + 1)
        gathered(r)
        own_copies[r].wait()
        for u in range(r * parts, (r + 1) * parts):
            compute(u)
            send_slots(u)
        if r == 0:
            for d in range(1, n):
                label_copy(d).wait_recv()
        while summed < r * parts:
            sum_slots(summed)
            summed += 1
    for u in range(summed, units):
        sum_slots(u)
    for u in range(units):
        finish(u)

    for r in range(chunks):
        for s in range(n - 1):
            @pl.when((me - s >= 0) & (me + 1 < n))
            def _():
                hop(r, s, True, me - s).wait_send()

            @pl.when((me + s <= n - 1) & (me > 0))
            def _():
                hop(r, s, False, me + s).wait_send()
        for d in range(1, n):
            sibling(r, lax.rem(me + d, n), core).wait_send()
    for u in range(units):
        for d in range(1, n):
            slot_copy(u, d).wait_send()
        for d in range(1, n_env):
            env_copy(u, d).wait_send()
    for d in range(1, n):
        label_copy(d).wait_send()


def on_device(n, n_env, wavefunction, left_env, right_env, left_index, out_sector):
    sectors, height, width = wavefunction.shape
    terms, blocks = left_env.shape[:2]
    outs = left_index.shape[-1]
    chunks = CHUNKS
    parts = PARTS
    units = chunks * parts
    span = height // chunks
    rows = span // parts
    pairs = terms * sectors * outs
    per = terms * blocks
    bf16, f32 = jnp.bfloat16, jnp.float32
    left = left_env.reshape(per, chunks, 2, span // 2, height)
    vmem = pl.BlockSpec(memory_space=pltpu.VMEM)
    hbm = pl.BlockSpec(memory_space=pltpu.HBM)
    dma = pltpu.SemaphoreType.DMA
    scratch = [
        pltpu.VMEM((2, sectors, height, width), bf16),
        pltpu.VMEM(right_env.shape, bf16),
        pltpu.VMEM((terms * sectors, height, width), bf16),
        pltpu.VMEM((pairs + 1, rows, width), f32),
        pltpu.VMEM((n, SLOTS, 8, 128), jnp.int32),
        pltpu.VMEM((n, SLOTS, 8, 128), jnp.int32),
        pltpu.VMEM((units, sectors, rows, width), f32),
        pltpu.SMEM((pairs,), jnp.int32),
        pltpu.SMEM((n * sectors,), jnp.int32),
        pltpu.SMEM(left_index.shape, jnp.int32),
        pltpu.SMEM(left_index.shape, jnp.int32),
        pltpu.SMEM((pairs,), jnp.int32),
        pltpu.SMEM((pairs,), jnp.int32),
    ]
    scratch += [pltpu.VMEM((n * per, 2, span // 2, height), bf16)] * chunks
    scratch += [pltpu.VMEM((n * SLOTS, rows, width), bf16)] * (2 * units)
    scratch += [pltpu.VMEM((n_env, sectors, rows, width), bf16)] * units
    scratch += [dma((chunks, n - 1))] * 4 + [dma((chunks, n))] * 2 + [dma, dma]
    scratch += [dma((units, n))] * 2 + [dma((n,))] * 2 + [dma((units, n_env))] * 2 + [dma((chunks + 4,))]
    dims = (n, n_env, chunks, parts, terms, sectors, blocks, outs)
    return pl.pallas_call(
        functools.partial(kernel, dims),
        out_shape=jax.ShapeDtypeStruct(wavefunction.shape, f32),
        in_specs=[hbm] * 5,
        out_specs=vmem,
        scratch_shapes=scratch,
        compiler_params=pltpu.CompilerParams(
            collective_id=0, has_side_effects=True, vmem_limit_bytes=63 * 1024 * 1024
        ),
    )(wavefunction, left, right_env, left_index, out_sector)


def solution(mesh):
    in_specs = (
        P(("groups", "sec"), None, "rep"),
        P(("groups", "env"), "sec", None, None),
        P(("groups", "env"), "sec", "rep", None),
        P(("groups", "env"), "sec", None),
        P(("groups", "env"), "sec", None),
    )
    out_specs = P(("groups", "sec"), None, "rep")
    return jax.shard_map(
        functools.partial(on_device, mesh.shape["sec"], mesh.shape["env"]),
        mesh=mesh,
        in_specs=in_specs,
        out_specs=out_specs,
        check_vma=False,
    )
```

```python
import functools

import jax
import jax.numpy as jnp
from jax import lax
from jax.experimental import pallas as pl
from jax.experimental.pallas import tpu as pltpu
from jax.sharding import PartitionSpec as P

MESH = pl.DeviceIdType.MESH
SLOTS = 2
CHUNKS = 1
PARTS = 4
PIECES = 2


def kernel(dims, *refs):
    n, n_env, chunks, parts, terms, sectors, blocks, outs = dims
    units = chunks * parts
    wave_ref, left_ref, right_hbm, lidx_in, osec_in, out_ref = refs[:6]
    refs = list(refs[6:])
    wave_all, right_ref, prods, chain, lab_send, lab_recv, dense_own, prev_s, last_s, lidx_s, osec_s, lidx_ref, osec_ref = refs[:13]
    refs = refs[13:]
    left_all = refs[:chunks]
    refs = refs[chunks:]
    slot_send = refs[:units]
    slot_recv = refs[units : 2 * units]
    env_all = refs[2 * units : 3 * units]
    (up_s, up_r, dn_s, dn_r, sib_s, sib_r, w_s, w_r, sl_s, sl_r, lb_s, lb_r, ev_s, ev_r, loc) = refs[3 * units :]
    me = lax.axis_index("sec")
    env = lax.axis_index("env")
    core = lax.axis_index("rep")
    per = terms * blocks
    pairs = terms * sectors * outs
    rows = left_ref.shape[2] * left_ref.shape[3] // parts
    width = wave_ref.shape[-1]

    barrier = pltpu.get_barrier_semaphore()
    for d in range(1, n):
        pl.semaphore_signal(barrier, inc=1, device_id={"sec": lax.rem(me + d, n)}, device_id_type=MESH)
    for d in range(1, n_env):
        pl.semaphore_signal(barrier, inc=1, device_id={"env": lax.rem(env + d, n_env)}, device_id_type=MESH)
    pl.semaphore_signal(barrier, inc=1, device_id={"rep": 1 - core}, device_id_type=MESH)
    pl.semaphore_wait(barrier, n - 1 + n_env - 1 + 1)

    def remote(src, dst, send, recv, where):
        return pltpu.make_async_remote_copy(
            src_ref=src, dst_ref=dst, send_sem=send, recv_sem=recv, device_id=where, device_id_type=MESH
        )

    part = per // PIECES

    def piece(r, q, origin):
        return left_all[r].at[pl.ds(origin * per + q * part, part), core]

    def hop(r, q, s, up, origin):
        src = left_ref.at[pl.ds(q * part, part), r, core] if s == 0 else piece(r, q, origin)
        send, recv = (up_s, up_r) if up else (dn_s, dn_r)
        where = jnp.minimum(me + 1, n - 1) if up else jnp.maximum(me - 1, 0)
        return remote(src, piece(r, q, origin), send.at[r * PIECES + q, s], recv.at[r * PIECES + q, s], {"sec": where})

    def sibling(r, q, origin, half):
        ref = left_all[r].at[pl.ds(origin * per + q * part, part), half]
        at = r * PIECES + q
        return remote(ref, ref, sib_s.at[at, origin], sib_r.at[at, origin], {"rep": 1 - core})

    def begin(r):
        @pl.when(me + 1 < n)
        def _():
            for q in range(PIECES):
                hop(r, q, 0, True, me).start()

        @pl.when(me > 0)
        def _():
            for q in range(PIECES):
                hop(r, q, 0, False, me).start()

    def pass_on(r, q, s, up):
        origin = me - 1 - s if up else me + 1 + s

        @pl.when((origin >= 0) & (origin <= n - 1))
        def _():
            hop(r, q, s, up, origin).wait_recv()
            if s + 1 <= n - 2:
                @pl.when((me + 1 < n) if up else (me > 0))
                def _():
                    hop(r, q, s + 1, up, origin).start()
            sibling(r, q, origin, core).start()

    def relay(r):
        for s in range(n - 1):
            for q in range(PIECES):
                pass_on(r, q, s, True)
                pass_on(r, q, s, False)

    def gathered(r):
        for d in range(1, n):
            for q in range(PIECES):
                sibling(r, q, lax.rem(me + d, n), 1 - core).wait_recv()

    begin(0)
    wave_copy = remote(wave_ref, wave_all.at[core], w_s, w_r, {"rep": 1 - core})
    wave_copy.start()
    own_copies = [
        pltpu.make_async_copy(left_ref.at[:, r], left_all[r].at[pl.ds(me * per, per)], loc.at[r])
        for r in range(chunks)
    ]
    for copy in own_copies:
        copy.start()
    in_copies = [
        pltpu.make_async_copy(wave_ref, wave_all.at[core], loc.at[chunks]),
        pltpu.make_async_copy(right_hbm, right_ref, loc.at[chunks + 1]),
    ]
    index_copies = [
        pltpu.make_async_copy(lidx_in, lidx_s, loc.at[chunks + 2]),
        pltpu.make_async_copy(osec_in, osec_s, loc.at[chunks + 3]),
    ]
    for copy in index_copies + in_copies:
        copy.start()
    for copy in index_copies:
        copy.wait()
    for p in range(pairs):
        k, s, m = p // (sectors * outs), p // outs % sectors, p % outs
        lidx_ref[p] = lidx_s[k, s, m]
        osec_ref[p] = osec_s[k, s, m]

    def find_prev(p, carry):
        target = osec_ref[p]
        found = jnp.int32(pairs)
        for q in range(pairs - 1):
            found = jnp.where((osec_ref[q] == target) & (q < p), q, found)
        prev_s[p] = found
        return carry

    lax.fori_loop(0, pairs, find_prev, 0)

    def find_last(v, carry):
        found = jnp.int32(-1)
        for q in range(pairs):
            found = jnp.where(osec_ref[q] == v, q, found)
        last_s[v] = found
        return carry

    lax.fori_loop(0, n * sectors, find_last, 0)

    def slot_of(owner, i):
        low, high = jnp.int32(-1), jnp.int32(-1)
        for l in range(sectors):
            here = last_s[owner * sectors + l] >= 0
            high = jnp.where(here, l, high)
            low = jnp.where(here & (low < 0), l, low)
        label = low if i == 0 else jnp.where(high == low, -1, high)
        source = jnp.where(label >= 0, last_s[owner * sectors + jnp.maximum(label, 0)], pairs)
        return label, source

    def write_labels(owner, carry):
        for i in range(SLOTS):
            lab_send[owner, i] = jnp.full((8, 128), slot_of(owner, i)[0], jnp.int32)
        return carry

    lax.fori_loop(0, n, write_labels, 0)

    def label_copy(d):
        owner = lax.rem(me + d, n)
        return remote(lab_send.at[owner], lab_recv.at[me], lb_s.at[d], lb_r.at[d], {"sec": owner})

    for d in range(1, n):
        label_copy(d).start()
    wave_copy.wait()
    for copy in in_copies:
        copy.wait()

    for s in range(sectors):
        wave = jnp.concatenate([wave_all[0, s], wave_all[1, s]], axis=-1)
        for k in range(terms):
            prods[k * sectors + s] = lax.dot_general(
                wave, right_ref[k, s], (((1,), (1,)), ((), ())), preferred_element_type=jnp.float32
            ).astype(jnp.bfloat16)
    chain[pairs] = jnp.zeros((rows, width), jnp.float32)

    def compute(u):
        r, t = u // parts, u % parts
        def body(ks, carry):
            k = ks // sectors
            right = prods[ks]
            lefts = []
            for m in range(outs):
                b = lidx_ref[ks * outs + m]
                left = left_all[r][(b // blocks) * per + k * blocks + lax.rem(b, blocks)]
                lefts.append(left.reshape(rows * parts, -1)[t * rows : (t + 1) * rows])
            values = jnp.dot(jnp.concatenate(lefts, axis=0), right, preferred_element_type=jnp.float32)
            for m in range(outs):
                p = ks * outs + m
                chain[p] = values[m * rows : (m + 1) * rows] + chain[prev_s[p]]
            return carry

        lax.fori_loop(0, terms * sectors, body, 0)

    def slot_copy(r, d):
        owner = lax.rem(me + d, n)
        return remote(
            slot_send[r].at[pl.ds(owner * SLOTS, SLOTS)],
            slot_recv[r].at[pl.ds(me * SLOTS, SLOTS)],
            sl_s.at[r, d],
            sl_r.at[r, d],
            {"sec": owner},
        )

    def send_slots(r):
        for d in range(1, n):
            owner = lax.rem(me + d, n)
            for i in range(SLOTS):
                slot_send[r][owner * SLOTS + i] = chain[slot_of(owner, i)[1]].astype(jnp.bfloat16)
            slot_copy(r, d).start()
        labels = [slot_of(me, i) for i in range(SLOTS)]
        parts = [chain[source] for _, source in labels]
        for l in range(sectors):
            total = jnp.zeros((rows, width), jnp.float32)
            for i in range(SLOTS):
                total = total + jnp.where(labels[i][0] == l, parts[i], 0.0)
            dense_own[r, l] = total

    def env_copy(r, d):
        peer = lax.rem(env + d, n_env)
        return remote(env_all[r], out_ref.at[env, :, pl.ds(r * rows, rows)], ev_s.at[r, d], ev_r.at[r, d], {"env": peer})

    def own_part(r):
        return pltpu.make_async_copy(env_all[r], out_ref.at[env, :, pl.ds(r * rows, rows)], ev_s.at[r, 0])

    def sum_slots(r):
        for d in range(1, n):
            slot_copy(r, d).wait_recv()
        for l in range(sectors):
            total = dense_own[r, l]
            for d in range(1, n):
                source = lax.rem(me + d, n)
                for i in range(SLOTS):
                    mask = lab_recv[source, i][:1] == l
                    total = total + jnp.where(mask, slot_recv[r][source * SLOTS + i].astype(jnp.float32), 0.0)
            env_all[r][l] = total.astype(env_all[r].dtype)
        for d in range(1, n_env):
            env_copy(r, d).start()
        own_part(r).start()

    def finish(r):
        for d in range(1, n_env):
            env_copy(r, d).wait_recv()
        own_part(r).wait()

    summed = 0
    for r in range(chunks):
        relay(r)
        if r + 1 < chunks:
            begin(r + 1)
        gathered(r)
        own_copies[r].wait()
        for u in range(r * parts, (r + 1) * parts):
            compute(u)
            send_slots(u)
        if r == 0:
            for d in range(1, n):
                label_copy(d).wait_recv()
        while summed < r * parts:
            sum_slots(summed)
            summed += 1
    for u in range(summed, units):
        sum_slots(u)
    for u in range(units):
        finish(u)

    for r in range(chunks):
        for s in range(n - 1):
            @pl.when((me - s >= 0) & (me + 1 < n))
            def _():
                for q in range(PIECES):
                    hop(r, q, s, True, me - s).wait_send()

            @pl.when((me + s <= n - 1) & (me > 0))
            def _():
                for q in range(PIECES):
                    hop(r, q, s, False, me + s).wait_send()
        for d in range(1, n):
            for q in range(PIECES):
                sibling(r, q, lax.rem(me + d, n), core).wait_send()
    for u in range(units):
        for d in range(1, n):
            slot_copy(u, d).wait_send()
        for d in range(1, n_env):
            env_copy(u, d).wait_send()
    for d in range(1, n):
        label_copy(d).wait_send()


def on_device(n, n_env, wavefunction, left_env, right_env, left_index, out_sector):
    sectors, height, width = wavefunction.shape
    terms, blocks = left_env.shape[:2]
    outs = left_index.shape[-1]
    chunks = CHUNKS
    parts = PARTS
    units = chunks * parts
    span = height // chunks
    rows = span // parts
    pairs = terms * sectors * outs
    per = terms * blocks
    bf16, f32 = jnp.bfloat16, jnp.float32
    left = left_env.reshape(per, chunks, 2, span // 2, height)
    hbm = pl.BlockSpec(memory_space=pltpu.HBM)
    dma = pltpu.SemaphoreType.DMA
    scratch = [
        pltpu.VMEM((2, sectors, height, width), bf16),
        pltpu.VMEM(right_env.shape, bf16),
        pltpu.VMEM((terms * sectors, height, width), bf16),
        pltpu.VMEM((pairs + 1, rows, width), f32),
        pltpu.VMEM((n, SLOTS, 8, 128), jnp.int32),
        pltpu.VMEM((n, SLOTS, 8, 128), jnp.int32),
        pltpu.VMEM((units, sectors, rows, width), f32),
        pltpu.SMEM((pairs,), jnp.int32),
        pltpu.SMEM((n * sectors,), jnp.int32),
        pltpu.SMEM(left_index.shape, jnp.int32),
        pltpu.SMEM(left_index.shape, jnp.int32),
        pltpu.SMEM((pairs,), jnp.int32),
        pltpu.SMEM((pairs,), jnp.int32),
    ]
    scratch += [pltpu.VMEM((n * per, 2, span // 2, height), bf16)] * chunks
    scratch += [pltpu.VMEM((n * SLOTS, rows, width), bf16)] * (2 * units)
    scratch += [pltpu.VMEM((sectors, rows, width), bf16)] * units
    scratch += [dma((chunks * PIECES, n - 1))] * 4 + [dma((chunks * PIECES, n))] * 2 + [dma, dma]
    scratch += [dma((units, n))] * 2 + [dma((n,))] * 2 + [dma((units, n_env))] * 2 + [dma((chunks + 4,))]
    dims = (n, n_env, chunks, parts, terms, sectors, blocks, outs)
    sums = pl.pallas_call(
        functools.partial(kernel, dims),
        out_shape=jax.ShapeDtypeStruct((n_env,) + wavefunction.shape, bf16),
        in_specs=[hbm] * 5,
        out_specs=hbm,
        scratch_shapes=scratch,
        compiler_params=pltpu.CompilerParams(
            collective_id=0, has_side_effects=True, vmem_limit_bytes=63 * 1024 * 1024
        ),
    )(wavefunction, left, right_env, left_index, out_sector)
    product = sums[0].astype(f32)
    for e in range(1, n_env):
        product = product + sums[e].astype(f32)
    return product


def solution(mesh):
    in_specs = (
        P(("groups", "sec"), None, "rep"),
        P(("groups", "env"), "sec", None, None),
        P(("groups", "env"), "sec", "rep", None),
        P(("groups", "env"), "sec", None),
        P(("groups", "env"), "sec", None),
    )
    out_specs = P(("groups", "sec"), None, "rep")
    return jax.shard_map(
        functools.partial(on_device, mesh.shape["sec"], mesh.shape["env"]),
        mesh=mesh,
        in_specs=in_specs,
        out_specs=out_specs,
        check_vma=False,
    )
```
